512 devices in a mesh: row: 32 (over y, z_lo), col: 8 (over x, core), rep: 2 (over z_hi).
Axes of the slice: x: 4, y: 4, z: 16 (z_hi: 2, z_lo: 8; z = z_hi * 8 + z_lo), core: 2. Of those that a mesh axis runs over, the one named last changes fastest.
Arguments:
- coeffs: bfloat16 [512, 98304], P('row', 'col'), may hold values from -6 to 6
- alpha_coupling: bfloat16 [512, 512], replicated, may hold values from -0.25 to 0.25
- parent_string_index: int32 [32, 98304], P('rep', 'col'), may hold values from 0 to 98303
- excitation_weight: float32 [32, 98304], P('rep', 'col'), may hold values from -1 to 1
Outputs:
- sigma: bfloat16 [512, 98304], P('row', 'col')
The draws below stay inside these ranges and needn't reach their ends.
Inputs may be any that keep to these rules, and one draw needn't show every extreme that they name: `parent_string_index`: global index of a beta string.
All inputs are finite; a program needn't handle non-finite values.
Results may differ from the reference program's by a relative error of at most 0.0012.
Values may be sent and summed in bfloat16 or wider, within the bound.
No kernel may reach another device: no remote copies, remote signals or barrier semaphores. Data moves between devices by JAX's collectives and lax.ppermute only.
A program may use at most 192 MiB of HBM per device.

```python
import jax
import jax.numpy as jnp
from jax import lax

SLOTS_PER_BETA = 32
ALPHA_STRINGS = 512
BETA_STRINGS = 98304


def touch_ends(values, stream_key, least, top_value):
    longest = values.shape.index(max(values.shape))
    spots = []
    for shift in (0, 1):
        where = [jax.random.randint(jax.random.fold_in(stream_key, axis), (), 0, length) for axis, length in enumerate(values.shape)]
        where[longest] = (where[longest] + shift) % values.shape[longest]
        spots.append(tuple(where))
    return values.at[spots[0]].set(least).at[spots[1]].set(top_value)


def block_levels(own_key, extent, split, smallest, high):
    loudness = 1.0
    for position, parts in split:
        steps = jax.random.uniform(jax.random.fold_in(jax.random.fold_in(own_key, 6), position), (parts,), jnp.float32, smallest / len(split), high / len(split))
        loudness = loudness * jnp.repeat(jnp.exp(steps), extent[position] // parts).reshape((-1,) + (1,) * (len(extent) - 1 - position))
    return loudness


def gaussian(stream_key, dims, deviation, most, split=(), dtype=jnp.bfloat16):
    array = deviation * jax.random.normal(stream_key, dims, jnp.float32)
    if split:
        array = array * block_levels(stream_key, dims, split, -0.22, 0.18)
    return jnp.clip(array, -most, most).astype(dtype)


def setup_inputs(seed: int = 0) -> dict:
    splits = jax.random.split(jax.random.key(seed), 5)
    coeffs = gaussian(splits[0], (ALPHA_STRINGS, BETA_STRINGS), 1.0, 6.0, ((0, 32), (1, 8)))
    alpha_coupling = gaussian(splits[1], (ALPHA_STRINGS, ALPHA_STRINGS), ALPHA_STRINGS ** -0.5, 0.25)
    parent_string_index = touch_ends(jax.random.randint(splits[2], (SLOTS_PER_BETA, BETA_STRINGS), 0, BETA_STRINGS), jax.random.fold_in(splits[2], 1), 0, BETA_STRINGS - 1).astype(jnp.int32)
    excitation_weight = gaussian(splits[3], (SLOTS_PER_BETA, BETA_STRINGS), SLOTS_PER_BETA ** -0.5, 1.0, ((0, 2), (1, 8)), jnp.float32)
    return dict(coeffs=coeffs, alpha_coupling=alpha_coupling, parent_string_index=parent_string_index, excitation_weight=excitation_weight)


def reference(coeffs, alpha_coupling, parent_string_index, excitation_weight):
    alpha_term = jnp.dot(alpha_coupling, coeffs, preferred_element_type=jnp.float32)

    def accumulate_slot(slot_index, running):
        sources = lax.dynamic_index_in_dim(parent_string_index, slot_index, 0, keepdims=False)
        weights = lax.dynamic_index_in_dim(excitation_weight, slot_index, 0, keepdims=False)
        picked = jnp.take(coeffs, sources, axis=1).astype(jnp.float32)
        return running + weights[None, :] * picked

    beta_contribution = lax.fori_loop(0, SLOTS_PER_BETA, accumulate_slot, jnp.zeros((ALPHA_STRINGS, BETA_STRINGS), jnp.float32))
    return (alpha_term + beta_contribution).astype(jnp.bfloat16)
```

```python
import functools

import jax
import jax.numpy as jnp
from jax import lax
from jax.experimental import pallas as pl
from jax.experimental.pallas import tpu as pltpu
from jax.sharding import PartitionSpec as P

Y = 4
Z = 8
LANES = 128


def pack_kernel(in_ref, out_ref):
    alphas, betas = in_ref.shape
    groups = LANES // alphas
    rows = betas // groups
    for c in range(rows // LANES):
        parts = [in_ref[:, pl.ds(g * rows + c * LANES, LANES)] for g in range(groups)]
        tile = jnp.concatenate(parts, axis=0).astype(jnp.float32)
        out_ref[pl.ds(c * LANES, LANES), :] = tile.T.astype(out_ref.dtype)


def pack_rows(coeffs):
    alphas, betas = coeffs.shape
    return pl.pallas_call(
        pack_kernel,
        out_shape=jax.ShapeDtypeStruct((alphas * betas // LANES, LANES), coeffs.dtype),
        name="pack_rows",
    )(coeffs)


def beta_kernel(chunk, idx_ref, w_ref, alpha_ref, packed_ref, out_ref, table, stage, acc_ref, sems):
    classes, rows = packed_ref.shape[1:3]
    per_class = rows // chunk
    chunks = classes * per_class
    depth = stage.shape[0]
    groups = 8
    width = LANES // groups

    def fetch(c, slot):
        start = pl.multiple_of(lax.rem(c, per_class) * chunk, 16)
        return pltpu.make_async_copy(
            packed_ref.at[:, c // per_class, pl.ds(start, chunk), :], stage.at[slot], sems.at[slot]
        )

    @pl.when(pl.program_id(0) == 0)
    def build_table():
        piece = 32
        part = lax.rem(lax.broadcasted_iota(jnp.int32, (piece, LANES), 1) // width, Y)
        for c in range(depth - 1):
            fetch(c, c).start()

        @pl.loop(0, chunks)
        def _(c):
            slot = lax.rem(c, depth)

            @pl.when(c + depth - 1 < chunks)
            def _():
                fetch(c + depth - 1, lax.rem(c + depth - 1, depth)).start()

            fetch(c, slot).wait()
            first = (c // per_class) * (groups * rows) + lax.rem(c, per_class) * chunk

            @pl.loop(0, chunk // piece)
            def _(s):
                at = pl.multiple_of(s * piece, piece)
                turned = []
                for y in range(Y):
                    shard = stage[slot, y, pl.ds(at, piece), :].astype(jnp.float32)
                    turned.append(pltpu.roll(shard, width * y, 1) if y else shard)
                for g in range(Y):
                    mixed = turned[(Y - 1 - g) % Y]
                    for j in range(Y - 1):
                        mixed = jnp.where(part == j, turned[(j - g) % Y], mixed)
                    for group in (g, g + Y):
                        to = pl.multiple_of(first + group * rows + at, piece)
                        back = (LANES - width * group) % LANES
                        table[pl.ds(to, piece), :] = pltpu.roll(mixed, back, 1) if back else mixed

    slots = w_ref.shape[1]
    block = acc_ref.shape[0]
    lane_row = lax.broadcasted_iota(jnp.int32, (8, LANES), 0)

    @pl.loop(0, block // 8)
    def _(g):
        base = pl.multiple_of(g * 8, 8)
        weights = w_ref[pl.ds(base, 8), :]
        total = jnp.zeros((8, LANES), jnp.float32)
        for q in range(slots):
            picked = None
            for k in range(8):
                source = idx_ref[base + (q * block + k)]
                row = jnp.broadcast_to(table[pl.ds(source, 1), :], (8, LANES))
                picked = row if k == 0 else jnp.where(lane_row == k, row, picked)
            total = total + picked * weights[:, q : q + 1]
        acc_ref[pl.ds(base, 8), :] = total

    alphas = out_ref.shape[0]
    out_ref[...] = (alpha_ref[...] + acc_ref[...].T[:alphas, :]).astype(out_ref.dtype)


def sigma_block(idx, weights, alpha_term, packed, block=128, chunk=768, depth=4):
    targets, slots = weights.shape
    alphas = alpha_term.shape[0]
    _, classes, rows, _ = packed.shape
    betas = classes * rows * 8
    return pl.pallas_call(
        functools.partial(beta_kernel, chunk),
        grid=(targets // block,),
        in_specs=[
            pl.BlockSpec((slots * block,), lambda i: (i,), memory_space=pltpu.SMEM),
            pl.BlockSpec((block, slots), lambda i: (i, 0)),
            pl.BlockSpec((alphas, block), lambda i: (0, i)),
            pl.BlockSpec(memory_space=pl.ANY),
        ],
        out_specs=pl.BlockSpec((alphas, block), lambda i: (0, i)),
        out_shape=jax.ShapeDtypeStruct((alphas, targets), jnp.bfloat16),
        scratch_shapes=[
            pltpu.VMEM((betas, LANES), jnp.float32),
            pltpu.VMEM((depth, Y, chunk, LANES), jnp.bfloat16),
            pltpu.VMEM((block, LANES), jnp.float32),
            pltpu.SemaphoreType.DMA((depth,)),
        ],
        compiler_params=pltpu.CompilerParams(vmem_limit_bytes=56 * 2**20),
        cost_estimate=pl.CostEstimate(
            flops=2 * alphas * targets * slots,
            bytes_accessed=packed.size * 2 + targets * slots * 8 + alphas * targets * 6,
            transcendentals=0,
        ),
        name="sigma_block",
    )(idx, weights, alpha_term, packed)


def per_device(coeffs, alpha_coupling, parent_string_index, excitation_weight):
    own_rows, betas = coeffs.shape
    strings = alpha_coupling.shape[0]
    reps = lax.axis_size("rep")
    cols = lax.axis_size("col")
    parts = reps * Y
    part = betas // parts
    small = part // Z
    along_z = [[y * Z + z for z in range(Z)] for y in range(Y)]
    y_and_col = [[(y * Z + z) * cols + c for y in range(Y) for c in range(cols)] for z in range(Z)]
    row = lax.axis_index("row")
    rep = lax.axis_index("rep")
    mine = (rep * Y + row // Z) * part
    theirs = ((1 - rep) * Y + row // Z) * part

    packed = lax.all_gather(
        pack_rows(coeffs), ("row", "col"), axis=0, axis_index_groups=y_and_col
    ).reshape(Y, cols, -1, LANES)

    half = lax.dynamic_slice_in_dim(coeffs, rep * (Y * part), Y * part, 1)
    pieces = half.reshape(own_rows, Y * Z, small).transpose(1, 0, 2)
    columns = lax.all_to_all(pieces, "row", 0, 0).reshape(strings, small)
    alpha_term = jnp.dot(alpha_coupling, columns, preferred_element_type=jnp.float32)
    alpha_term = alpha_term.reshape(Y, Z, own_rows, small).transpose(1, 0, 2, 3)
    alpha_term = lax.all_to_all(alpha_term, "row", 0, 0, axis_index_groups=along_z)
    alpha_term = alpha_term.transpose(1, 2, 0, 3).reshape(Y * own_rows, part)

    swap = [(0, 1), (1, 0)]

    def all_slots(array):
        own = lax.dynamic_slice_in_dim(array, mine, part, 1)
        other = lax.ppermute(lax.dynamic_slice_in_dim(array, theirs, part, 1), "rep", swap)
        return jnp.concatenate([own, other], axis=0)

    idx = all_slots(parent_string_index)
    idx = idx.reshape(idx.shape[0], part // LANES, LANES).transpose(1, 0, 2).reshape(-1)
    weights = all_slots(excitation_weight).T

    sigma = sigma_block(idx, weights, alpha_term, packed)
    pieces = sigma.reshape(Y, own_rows, part)
    pieces = jnp.concatenate([pieces, pieces], axis=0)
    back = [[r * Y * Z + y * Z + z for r in range(reps) for y in range(Y)] for z in range(Z)]
    done = lax.all_to_all(pieces, ("rep", "row"), 0, 0, axis_index_groups=back, tiled=True)
    return done.reshape(parts, own_rows, part).transpose(1, 0, 2).reshape(own_rows, betas)


def solution(mesh):
    placed = (P("row", "col"), P(), P("rep", "col"), P("rep", "col"))
    return jax.shard_map(
        per_device, mesh=mesh, in_specs=placed, out_specs=P("row", "col"), check_vma=False
    )
```

```python
import functools

import jax
import jax.numpy as jnp
from jax import lax
from jax.experimental import pallas as pl
from jax.experimental.pallas import tpu as pltpu
from jax.sharding import PartitionSpec as P

Y = 4
Z = 8
LANES = 128


def pack_kernel(in_ref, out_ref):
    alphas, betas = in_ref.shape
    groups = LANES // alphas
    rows = betas // groups
    for c in range(rows // LANES):
        parts = [in_ref[:, pl.ds(g * rows + c * LANES, LANES)] for g in range(groups)]
        tile = jnp.concatenate(parts, axis=0).astype(jnp.float32)
        out_ref[pl.ds(c * LANES, LANES), :] = tile.T.astype(out_ref.dtype)


def pack_rows(coeffs):
    alphas, betas = coeffs.shape
    return pl.pallas_call(
        pack_kernel,
        out_shape=jax.ShapeDtypeStruct((alphas * betas // LANES, LANES), coeffs.dtype),
        name="pack_rows",
    )(coeffs)


def beta_kernel(
    chunk, idx_ref, w_ref, alpha_ref, packed_ref, out_ref, table, stage, spread, acc_ref, sems
):
    classes, rows = packed_ref.shape[1:3]
    per_class = rows // chunk
    chunks = classes * per_class
    depth = stage.shape[0]

    def fetch(c, slot):
        start = pl.multiple_of(lax.rem(c, per_class) * chunk, 16)
        return pltpu.make_async_copy(
            packed_ref.at[:, c // per_class, pl.ds(start, chunk), :], stage.at[slot], sems.at[slot]
        )

    @pl.when(pl.program_id(0) == 0)
    def build_table():
        for c in range(depth - 1):
            fetch(c, c).start()
        source = lax.broadcasted_iota(jnp.int32, spread.shape, 0)
        target = (
            ((source >> 4) & 3) * 128 + ((source >> 6) & 1) * 64 + (source >> 7) * 16 + (source & 15)
        )
        column = lax.broadcasted_iota(jnp.int32, spread.shape, 1)
        spread[...] = jnp.where(target == column, 1.0, 0.0).astype(spread.dtype)
        piece = 256

        @pl.loop(0, chunks)
        def _(c):
            slot = lax.rem(c, depth)

            @pl.when(c + depth - 1 < chunks)
            def _():
                fetch(c + depth - 1, lax.rem(c + depth - 1, depth)).start()

            fetch(c, slot).wait()
            first = (c // per_class) * (Y * rows) + lax.rem(c, per_class) * chunk
            for at in range(0, chunk, piece):
                shards = [stage[slot, y, pl.ds(at, piece), :] for y in range(Y)]
                mixed = jnp.dot(
                    jnp.concatenate(shards, axis=1), spread[...], preferred_element_type=jnp.float32
                )
                for g in range(Y):
                    to = pl.multiple_of(first + (g * rows + at), 8)
                    table[pl.ds(to, piece), :] = mixed[:, g * LANES : (g + 1) * LANES]

    slots = w_ref.shape[1] // 2
    block = acc_ref.shape[0]
    lane_row = lax.broadcasted_iota(jnp.int32, (8, LANES), 0)
    low_lane = lax.broadcasted_iota(jnp.int32, (8, LANES), 1) < LANES // 2

    @pl.loop(0, block // 8)
    def _(g):
        base = pl.multiple_of(g * 8, 8)
        weights = w_ref[pl.ds(base, 8), :]
        total = jnp.zeros((8, LANES), jnp.float32)
        for q in range(slots):
            picked = None
            for k in range(8):
                source = idx_ref[base + (q * block + k)]
                row = jnp.broadcast_to(table[pl.ds(source, 1), :], (8, LANES))
                picked = row if k == 0 else jnp.where(lane_row == k, row, picked)
            low = jnp.broadcast_to(weights[:, q : q + 1], (8, LANES))
            high = jnp.broadcast_to(weights[:, slots + q : slots + q + 1], (8, LANES))
            total = total + picked * jnp.where(low_lane, low, high)
        acc_ref[pl.ds(base, 8), :] = total

    alphas = out_ref.shape[0]
    turned = acc_ref[...].T
    beta_term = turned[:alphas, :] + turned[alphas:, :]
    out_ref[...] = (alpha_ref[...] + beta_term).astype(out_ref.dtype)


def sigma_block(idx, weights, alpha_term, packed, block=128, chunk=768, depth=4):
    targets, slots = weights.shape
    alphas = alpha_term.shape[0]
    _, classes, rows, _ = packed.shape
    pairs = classes * rows * Y
    return pl.pallas_call(
        functools.partial(beta_kernel, chunk),
        grid=(targets // block,),
        in_specs=[
            pl.BlockSpec((slots // 2 * block,), lambda i: (i,), memory_space=pltpu.SMEM),
            pl.BlockSpec((block, slots), lambda i: (i, 0)),
            pl.BlockSpec((alphas, block), lambda i: (0, i)),
            pl.BlockSpec(memory_space=pl.ANY),
        ],
        out_specs=pl.BlockSpec((alphas, block), lambda i: (0, i)),
        out_shape=jax.ShapeDtypeStruct((alphas, targets), jnp.bfloat16),
        scratch_shapes=[
            pltpu.VMEM((pairs, LANES), jnp.float32),
            pltpu.VMEM((depth, Y, chunk, LANES), jnp.bfloat16),
            pltpu.VMEM((Y * LANES, Y * LANES), jnp.bfloat16),
            pltpu.VMEM((block, LANES), jnp.float32),
            pltpu.SemaphoreType.DMA((depth,)),
        ],
        compiler_params=pltpu.CompilerParams(vmem_limit_bytes=56 * 2**20),
        cost_estimate=pl.CostEstimate(
            flops=2 * alphas * targets * slots + 2 * pairs * LANES * Y * LANES,
            bytes_accessed=packed.size * 2 + targets * slots * 8 + alphas * targets * 6,
            transcendentals=0,
        ),
        name="sigma_block",
    )(idx, weights, alpha_term, packed)


def per_device(coeffs, alpha_coupling, parent_string_index, excitation_weight):
    own_rows, betas = coeffs.shape
    strings = alpha_coupling.shape[0]
    reps = lax.axis_size("rep")
    cols = lax.axis_size("col")
    parts = reps * Y
    part = betas // parts
    small = part // Z
    along_z = [[y * Z + z for z in range(Z)] for y in range(Y)]
    y_and_col = [[(y * Z + z) * cols + c for y in range(Y) for c in range(cols)] for z in range(Z)]
    row = lax.axis_index("row")
    rep = lax.axis_index("rep")
    mine = (rep * Y + row // Z) * part
    theirs = ((1 - rep) * Y + row // Z) * part

    packed = lax.all_gather(
        pack_rows(coeffs), ("row", "col"), axis=0, axis_index_groups=y_and_col
    ).reshape(Y, cols, -1, LANES)

    half = lax.dynamic_slice_in_dim(coeffs, rep * (Y * part), Y * part, 1)
    pieces = half.reshape(own_rows, Y * Z, small).transpose(1, 0, 2)
    columns = lax.all_to_all(pieces, "row", 0, 0).reshape(strings, small)
    alpha_term = jnp.dot(alpha_coupling, columns, preferred_element_type=jnp.float32)
    alpha_term = alpha_term.reshape(Y, Z, own_rows, small).transpose(1, 0, 2, 3)
    alpha_term = lax.all_to_all(alpha_term, "row", 0, 0, axis_index_groups=along_z)
    alpha_term = alpha_term.transpose(1, 2, 0, 3).reshape(Y * own_rows, part)

    swap = [(0, 1), (1, 0)]

    def all_slots(array):
        own = lax.dynamic_slice_in_dim(array, mine, part, 1)
        other = lax.ppermute(lax.dynamic_slice_in_dim(array, theirs, part, 1), "rep", swap)
        return jnp.concatenate([own, other], axis=0)

    idx = all_slots(parent_string_index)
    halves = idx // (betas // 2)
    idx = idx - ((halves + 1) // 2) * (betas // 2)
    idx = idx.reshape(idx.shape[0], part // LANES, LANES).transpose(1, 0, 2).reshape(-1)
    weights = all_slots(excitation_weight)
    upper = halves % 2 == 1
    weights = jnp.concatenate(
        [jnp.where(upper, 0.0, weights), jnp.where(upper, weights, 0.0)], axis=0
    ).T

    sigma = sigma_block(idx, weights, alpha_term, packed)
    pieces = sigma.reshape(Y, own_rows, part)
    pieces = jnp.concatenate([pieces, pieces], axis=0)
    back = [[r * Y * Z + y * Z + z for r in range(reps) for y in range(Y)] for z in range(Z)]
    done = lax.all_to_all(pieces, ("rep", "row"), 0, 0, axis_index_groups=back, tiled=True)
    return done.reshape(parts, own_rows, part).transpose(1, 0, 2).reshape(own_rows, betas)


def solution(mesh):
    placed = (P("row", "col"), P(), P("rep", "col"), P("rep", "col"))
    return jax.shard_map(
        per_device, mesh=mesh, in_specs=placed, out_specs=P("row", "col"), check_vma=False
    )
```

```python
import functools

import jax
import jax.numpy as jnp
from jax import lax
from jax.experimental import pallas as pl
from jax.experimental.pallas import tpu as pltpu
from jax.sharding import PartitionSpec as P

Y = 4
Z = 8
LANES = 128


def pack_kernel(in_ref, out_ref):
    alphas, betas = in_ref.shape
    groups = LANES // alphas
    rows = betas // groups
    for c in range(rows // LANES):
        parts = [in_ref[:, pl.ds(g * rows + c * LANES, LANES)] for g in range(groups)]
        tile = jnp.concatenate(parts, axis=0).astype(jnp.float32)
        out_ref[pl.ds(c * LANES, LANES), :] = tile.T.astype(out_ref.dtype)


def pack_rows(coeffs):
    alphas, betas = coeffs.shape
    return pl.pallas_call(
        pack_kernel,
        out_shape=jax.ShapeDtypeStruct((alphas * betas // LANES, LANES), coeffs.dtype),
        name="pack_rows",
    )(coeffs)


def beta_kernel(
    chunk,
    idx_ref, w_ref, alpha_ref, packed_ref, out_ref,
    table, stage, spread, acc_ref, near, sems, near_sems,
):
    classes, rows = packed_ref.shape[1:3]
    per_class = rows // chunk
    chunks = classes * per_class
    depth = stage.shape[0]
    buffers, batch, slots = near.shape
    targets = w_ref.shape[0]
    rounds = targets // (buffers * batch)

    def fetch(c, slot):
        start = pl.multiple_of(lax.rem(c, per_class) * chunk, 16)
        return pltpu.make_async_copy(
            packed_ref.at[:, c // per_class, pl.ds(start, chunk), :], stage.at[slot], sems.at[slot]
        )

    def bring(r, b):
        start = pl.multiple_of((r * buffers + b) * batch, batch)
        return pltpu.make_async_copy(
            idx_ref.at[pl.ds(start, batch), :], near.at[b], near_sems.at[b]
        )

    for c in range(depth - 1):
        fetch(c, c).start()
    for b in range(buffers):
        bring(0, b).start()

    source = lax.broadcasted_iota(jnp.int32, spread.shape, 0)
    target = (
        ((source >> 4) & 3) * 128 + ((source >> 6) & 1) * 64 + (source >> 7) * 16 + (source & 15)
    )
    column = lax.broadcasted_iota(jnp.int32, spread.shape, 1)
    spread[...] = jnp.where(target == column, 1.0, 0.0).astype(spread.dtype)
    piece = 256

    @pl.loop(0, chunks)
    def _(c):
        slot = lax.rem(c, depth)

        @pl.when(c + depth - 1 < chunks)
        def _():
            fetch(c + depth - 1, lax.rem(c + depth - 1, depth)).start()

        fetch(c, slot).wait()
        first = (c // per_class) * (Y * rows) + lax.rem(c, per_class) * chunk
        for at in range(0, chunk, piece):
            shards = [stage[slot, y, pl.ds(at, piece), :] for y in range(Y)]
            mixed = jnp.dot(
                jnp.concatenate(shards, axis=1), spread[...], preferred_element_type=jnp.float32
            )
            for g in range(Y):
                to = pl.multiple_of(first + (g * rows + at), 8)
                table[pl.ds(to, piece), :] = mixed[:, g * LANES : (g + 1) * LANES]

    lane_row = lax.broadcasted_iota(jnp.int32, (8, LANES), 0)
    low_lane = lax.broadcasted_iota(jnp.int32, (8, LANES), 1) < LANES // 2

    @pl.loop(0, rounds)
    def _(r):
        for b in range(buffers):
            bring(r, b).wait()
            for g in range(0, batch, 8):
                base = pl.multiple_of((r * buffers + b) * batch + g, 8)
                weights = w_ref[pl.ds(base, 8), :]
                total = jnp.zeros((8, LANES), jnp.float32)
                for q in range(slots):
                    picked = None
                    for k in range(8):
                        row = table[pl.ds(near[b, g + k, q], 1), :]
                        row = jnp.broadcast_to(row, (8, LANES))
                        picked = row if k == 0 else jnp.where(lane_row == k, row, picked)
                    low = jnp.broadcast_to(weights[:, q : q + 1], (8, LANES))
                    high = jnp.broadcast_to(weights[:, slots + q : slots + q + 1], (8, LANES))
                    total = total + picked * jnp.where(low_lane, low, high)
                acc_ref[pl.ds(base, 8), :] = total

            @pl.when(r + 1 < rounds)
            def _():
                bring(r + 1, b).start()

    alphas = out_ref.shape[0]
    for at in range(0, targets, LANES):
        turned = acc_ref[pl.ds(at, LANES), :].T
        beta_term = turned[:alphas, :] + turned[alphas:, :]
        total = alpha_ref[:, pl.ds(at, LANES)] + beta_term
        out_ref[:, pl.ds(at, LANES)] = total.astype(out_ref.dtype)


def sigma_block(idx, weights, alpha_term, packed, chunk=768, depth=4, buffers=4, batch=16):
    targets, slots = idx.shape
    alphas = alpha_term.shape[0]
    _, classes, rows, _ = packed.shape
    pairs = classes * rows * Y
    return pl.pallas_call(
        functools.partial(beta_kernel, chunk),
        in_specs=[
            pl.BlockSpec(memory_space=pl.ANY),
            pl.BlockSpec(memory_space=pltpu.VMEM),
            pl.BlockSpec(memory_space=pltpu.VMEM),
            pl.BlockSpec(memory_space=pl.ANY),
        ],
        out_specs=pl.BlockSpec(memory_space=pltpu.VMEM),
        out_shape=jax.ShapeDtypeStruct((alphas, targets), jnp.bfloat16),
        scratch_shapes=[
            pltpu.VMEM((pairs, LANES), jnp.float32),
            pltpu.VMEM((depth, Y, chunk, LANES), jnp.bfloat16),
            pltpu.VMEM((Y * LANES, Y * LANES), jnp.bfloat16),
            pltpu.VMEM((targets, LANES), jnp.float32),
            pltpu.SMEM((buffers, batch, slots), jnp.int32),
            pltpu.SemaphoreType.DMA((depth,)),
            pltpu.SemaphoreType.DMA((buffers,)),
        ],
        compiler_params=pltpu.CompilerParams(vmem_limit_bytes=56 * 2**20),
        cost_estimate=pl.CostEstimate(
            flops=2 * alphas * targets * slots + 2 * pairs * LANES * Y * LANES,
            bytes_accessed=packed.size * 2 + targets * slots * 8 + alphas * targets * 6,
            transcendentals=0,
        ),
        name="sigma_block",
    )(idx, weights, alpha_term, packed)


def per_device(coeffs, alpha_coupling, parent_string_index, excitation_weight):
    own_rows, betas = coeffs.shape
    strings = alpha_coupling.shape[0]
    reps = lax.axis_size("rep")
    cols = lax.axis_size("col")
    parts = reps * Y
    part = betas // parts
    small = part // Z
    along_z = [[y * Z + z for z in range(Z)] for y in range(Y)]
    y_and_col = [[(y * Z + z) * cols + c for y in range(Y) for c in range(cols)] for z in range(Z)]
    row = lax.axis_index("row")
    rep = lax.axis_index("rep")
    mine = (rep * Y + row // Z) * part
    theirs = ((1 - rep) * Y + row // Z) * part

    packed = lax.all_gather(
        pack_rows(coeffs), ("row", "col"), axis=0, axis_index_groups=y_and_col
    ).reshape(Y, cols, -1, LANES)

    half = lax.dynamic_slice_in_dim(coeffs, rep * (Y * part), Y * part, 1)
    pieces = half.reshape(own_rows, Y * Z, small).transpose(1, 0, 2)
    columns = lax.all_to_all(pieces, "row", 0, 0).reshape(strings, small)
    alpha_term = jnp.dot(alpha_coupling, columns, preferred_element_type=jnp.float32)
    alpha_term = alpha_term.reshape(Y, Z, own_rows, small).transpose(1, 0, 2, 3)
    alpha_term = lax.all_to_all(alpha_term, "row", 0, 0, axis_index_groups=along_z)
    alpha_term = alpha_term.transpose(1, 2, 0, 3).reshape(Y * own_rows, part)

    swap = [(0, 1), (1, 0)]

    def all_slots(array):
        own = lax.dynamic_slice_in_dim(array, mine, part, 1)
        other = lax.ppermute(lax.dynamic_slice_in_dim(array, theirs, part, 1), "rep", swap)
        return jnp.concatenate([own, other], axis=0)

    idx = all_slots(parent_string_index)
    halves = idx // (betas // 2)
    idx = idx - ((halves + 1) // 2) * (betas // 2)
    idx = idx.T
    weights = all_slots(excitation_weight)
    upper = halves % 2 == 1
    weights = jnp.concatenate(
        [jnp.where(upper, 0.0, weights), jnp.where(upper, weights, 0.0)], axis=0
    ).T

    sigma = sigma_block(idx, weights, alpha_term, packed)
    pieces = sigma.reshape(Y, own_rows, part)
    pieces = jnp.concatenate([pieces, pieces], axis=0)
    back = [[r * Y * Z + y * Z + z for r in range(reps) for y in range(Y)] for z in range(Z)]
    done = lax.all_to_all(pieces, ("rep", "row"), 0, 0, axis_index_groups=back, tiled=True)
    return done.reshape(parts, own_rows, part).transpose(1, 0, 2).reshape(own_rows, betas)


def solution(mesh):
    placed = (P("row", "col"), P(), P("rep", "col"), P("rep", "col"))
    return jax.shard_map(
        per_device, mesh=mesh, in_specs=placed, out_specs=P("row", "col"), check_vma=False
    )
```

```python
import functools

import jax
import jax.numpy as jnp
from jax import lax
from jax.experimental import pallas as pl
from jax.experimental.pallas import tpu as pltpu
from jax.sharding import PartitionSpec as P

Y = 4
Z = 8
LANES = 128


def pack_kernel(turn_ref, in_ref, out_ref):
    alphas, betas = in_ref.shape
    groups = LANES // alphas
    rows = betas // groups
    for c in range(rows // LANES):
        parts = []
        for block in range(groups):
            group = lax.rem(block + groups - turn_ref[0], groups)
            start = pl.multiple_of(group * rows + c * LANES, LANES)
            parts.append(in_ref[:, pl.ds(start, LANES)])
        tile = jnp.concatenate(parts, axis=0).astype(jnp.float32)
        out_ref[pl.ds(c * LANES, LANES), :] = tile.T.astype(out_ref.dtype)


def pack_rows(coeffs, turn):
    alphas, betas = coeffs.shape
    return pl.pallas_call(
        pack_kernel,
        in_specs=[
            pl.BlockSpec(memory_space=pltpu.SMEM),
            pl.BlockSpec(memory_space=pltpu.VMEM),
        ],
        out_specs=pl.BlockSpec(memory_space=pltpu.VMEM),
        out_shape=jax.ShapeDtypeStruct((alphas * betas // LANES, LANES), coeffs.dtype),
        name="pack_rows",
    )(turn.reshape(1), coeffs)


def beta_kernel(
    chunk,
    idx_ref, w_ref, own_ref, other_ref, out_ref,
    table, stage, spread, acc_ref, near, sems, near_sems,
):
    _, classes, rows, _ = own_ref.shape
    per_class = rows // chunk
    chunks = classes * per_class
    depth = stage.shape[0]
    buffers, batch, slots = near.shape
    targets = w_ref.shape[0]
    rounds = targets // (buffers * batch)

    def fetch(packed_ref, c, slot):
        start = pl.multiple_of(lax.rem(c, per_class) * chunk, 16)
        return pltpu.make_async_copy(
            packed_ref.at[:, c // per_class, pl.ds(start, chunk), :], stage.at[slot], sems.at[slot]
        )

    def bring(r, b):
        start = pl.multiple_of((r * buffers + b) * batch, batch)
        return pltpu.make_async_copy(
            idx_ref.at[pl.ds(start, batch), :], near.at[b], near_sems.at[b]
        )

    for c in range(depth - 1):
        fetch(own_ref, c, c).start()
    for b in range(buffers):
        bring(0, b).start()

    size = 2 * LANES
    source = lax.broadcasted_iota(jnp.int32, (size, size), 0)
    column = lax.broadcasted_iota(jnp.int32, (size, size), 1)
    for m in range(Y // 2):
        turn = 2 * m + (column >> 7)
        wanted = (column & 128) + ((column + 16 * turn) & 127)
        spread[m] = jnp.where(source == wanted, 1.0, 0.0).astype(spread.dtype)
    piece = 256
    lane_part = (lax.broadcasted_iota(jnp.int32, (piece, LANES), 1) >> 4) & 3

    @pl.loop(0, 2 * chunks)
    def _(c):
        slot = lax.rem(c, depth)
        ahead = c + depth - 1

        @pl.when(ahead < chunks)
        def _():
            fetch(own_ref, ahead, lax.rem(ahead, depth)).start()

        @pl.when(jnp.logical_and(ahead >= chunks, ahead < 2 * chunks))
        def _():
            fetch(other_ref, ahead - chunks, lax.rem(ahead, depth)).start()

        fetch(own_ref, lax.rem(c, chunks), slot).wait()
        first = (c // per_class) * (Y * rows) + lax.rem(c, per_class) * chunk
        for at in range(0, chunk, piece):
            shards = [stage[slot, y, pl.ds(at, piece), :] for y in range(Y)]
            mixed = []
            for g in range(Y):
                rows_g = shards[(Y - 1 - g) % Y]
                for j in range(Y - 1):
                    rows_g = jnp.where(lane_part == j, shards[(j - g) % Y], rows_g)
                mixed.append(rows_g)
            for m in range(Y // 2):
                turned = jnp.dot(
                    jnp.concatenate(mixed[2 * m : 2 * m + 2], axis=1),
                    spread[m],
                    preferred_element_type=jnp.float32,
                )
                for g in (2 * m, 2 * m + 1):
                    to = pl.multiple_of(first + (g * rows + at), 8)
                    lanes = (g - 2 * m) * LANES
                    table[pl.ds(to, piece), :] = turned[:, lanes : lanes + LANES]

    lane_row = lax.broadcasted_iota(jnp.int32, (8, LANES), 0)
    low_lane = lax.broadcasted_iota(jnp.int32, (8, LANES), 1) < LANES // 2

    @pl.loop(0, rounds)
    def _(r):
        for b in range(buffers):
            bring(r, b).wait()
            for g in range(0, batch, 8):
                base = pl.multiple_of((r * buffers + b) * batch + g, 8)
                weights = w_ref[pl.ds(base, 8), :]
                total = jnp.zeros((8, LANES), jnp.float32)
                for q in range(slots):
                    picked = None
                    for k in range(8):
                        row = table[pl.ds(near[b, g + k, q], 1), :]
                        row = jnp.broadcast_to(row, (8, LANES))
                        picked = row if k == 0 else jnp.where(lane_row == k, row, picked)
                    low = jnp.broadcast_to(weights[:, q : q + 1], (8, LANES))
                    high = jnp.broadcast_to(weights[:, slots + q : slots + q + 1], (8, LANES))
                    total = total + picked * jnp.where(low_lane, low, high)
                acc_ref[pl.ds(base, 8), :] = total

            @pl.when(r + 1 < rounds)
            def _():
                bring(r + 1, b).start()

    alphas = out_ref.shape[0]
    for at in range(0, targets, LANES):
        turned = acc_ref[pl.ds(at, LANES), :].T
        out_ref[:, pl.ds(at, LANES)] = turned[:alphas, :] + turned[alphas:, :]


def beta_block(idx, weights, own, other, chunk=768, depth=4, buffers=2, batch=32):
    targets, slots = idx.shape
    _, classes, rows, _ = own.shape
    pairs = 2 * classes * rows * Y
    alphas = LANES // 2
    return pl.pallas_call(
        functools.partial(beta_kernel, chunk),
        in_specs=[
            pl.BlockSpec(memory_space=pl.ANY),
            pl.BlockSpec(memory_space=pltpu.VMEM),
            pl.BlockSpec(memory_space=pl.ANY),
            pl.BlockSpec(memory_space=pl.ANY),
        ],
        out_specs=pl.BlockSpec(memory_space=pltpu.VMEM),
        out_shape=jax.ShapeDtypeStruct((alphas, targets), jnp.float32),
        scratch_shapes=[
            pltpu.VMEM((pairs, LANES), jnp.float32),
            pltpu.VMEM((depth, Y, chunk, LANES), jnp.bfloat16),
            pltpu.VMEM((Y // 2, 2 * LANES, 2 * LANES), jnp.bfloat16),
            pltpu.VMEM((targets, LANES), jnp.float32),
            pltpu.SMEM((buffers, batch, slots), jnp.int32),
            pltpu.SemaphoreType.DMA((depth,)),
            pltpu.SemaphoreType.DMA((buffers,)),
        ],
        compiler_params=pltpu.CompilerParams(vmem_limit_bytes=36 * 2**20),
        cost_estimate=pl.CostEstimate(
            flops=2 * pairs * LANES * Y * LANES,
            bytes_accessed=pairs * LANES * 2 + targets * slots * 8 + alphas * targets * 4,
            transcendentals=0,
        ),
        name="beta_block",
    )(idx, weights, own, other)


def per_device(coeffs, alpha_coupling, parent_string_index, excitation_weight):
    own_rows, betas = coeffs.shape
    strings = alpha_coupling.shape[0]
    reps = lax.axis_size("rep")
    cols = lax.axis_size("col")
    parts = reps * Y
    part = betas // parts
    small = part // Z
    along_z = [[y * Z + z for z in range(Z)] for y in range(Y)]
    y_and_x = [
        [(y * Z + z) * cols + 2 * x + core for y in range(Y) for x in range(cols // 2)]
        for z in range(Z)
        for core in range(2)
    ]
    row = lax.axis_index("row")
    rep = lax.axis_index("rep")
    core = lax.axis_index("col") % 2
    mine = (rep * Y + row // Z) * part
    theirs = ((1 - rep) * Y + row // Z) * part

    own = lax.all_gather(
        pack_rows(coeffs, row // Z), ("row", "col"), axis=0, axis_index_groups=y_and_x
    ).reshape(Y, cols // 2, -1, LANES)

    half = lax.dynamic_slice_in_dim(coeffs, rep * (Y * part), Y * part, 1)
    pieces = half.reshape(own_rows, Y * Z, small).transpose(1, 0, 2)
    columns = lax.all_to_all(pieces, "row", 0, 0).reshape(strings, small)
    alpha_term = jnp.dot(alpha_coupling, columns, preferred_element_type=jnp.float32)
    alpha_term = alpha_term.reshape(Y, Z, own_rows, small).transpose(1, 0, 2, 3)

    sent = jnp.concatenate(
        [
            lax.dynamic_slice_in_dim(parent_string_index, theirs, part, 1).astype(jnp.float32),
            lax.dynamic_slice_in_dim(excitation_weight, theirs, part, 1),
        ],
        axis=0,
    )
    got = lax.ppermute(sent, "rep", [(0, 1), (1, 0)])
    slots = parent_string_index.shape[0]
    idx = jnp.concatenate(
        [
            lax.dynamic_slice_in_dim(parent_string_index, mine, part, 1),
            got[:slots].astype(jnp.int32),
        ],
        axis=0,
    )
    weights = jnp.concatenate(
        [lax.dynamic_slice_in_dim(excitation_weight, mine, part, 1), got[slots:]], axis=0
    )
    halves = idx // (betas // 2)
    place = (((halves >> 1) & 1) ^ core) * (cols // 2) + (halves >> 2)
    upper = (halves & 1) == 1
    idx = (idx + (place - halves) * (betas // 2)).T
    weights = jnp.concatenate(
        [jnp.where(upper, 0.0, weights), jnp.where(upper, weights, 0.0)], axis=0
    ).T

    own, idx, weights, alpha_term = lax.optimization_barrier((own, idx, weights, alpha_term))
    other = lax.ppermute(own, "col", [(c, c ^ 1) for c in range(cols)])
    alpha_term = lax.all_to_all(alpha_term, "row", 0, 0, axis_index_groups=along_z)
    alpha_term = alpha_term.transpose(1, 2, 0, 3).reshape(Y * own_rows, part)

    beta_term = beta_block(idx, weights, own, other)
    sigma = (alpha_term + beta_term).astype(jnp.bfloat16)
    pieces = sigma.reshape(Y, own_rows, part)
    pieces = jnp.concatenate([pieces, pieces], axis=0)
    back = [[r * Y * Z + y * Z + z for r in range(reps) for y in range(Y)] for z in range(Z)]
    done = lax.all_to_all(pieces, ("rep", "row"), 0, 0, axis_index_groups=back, tiled=True)
    return done.reshape(parts, own_rows, part).transpose(1, 0, 2).reshape(own_rows, betas)


def solution(mesh):
    placed = (P("row", "col"), P(), P("rep", "col"), P("rep", "col"))
    return jax.shard_map(
        per_device, mesh=mesh, in_specs=placed, out_specs=P("row", "col"), check_vma=False
    )
```

```python
import functools

import jax
import jax.numpy as jnp
from jax import lax
from jax.experimental import pallas as pl
from jax.experimental.pallas import tpu as pltpu
from jax.sharding import PartitionSpec as P

Y = 4
Z = 8
LANES = 128


def pack_kernel(turn_ref, in_ref, out_ref):
    alphas, betas = in_ref.shape
    groups = LANES // alphas
    rows = betas // groups
    for c in range(rows // LANES):
        parts = []
        for block in range(groups):
            group = lax.rem(block + groups - turn_ref[0], groups)
            start = pl.multiple_of(group * rows + c * LANES, LANES)
            parts.append(in_ref[:, pl.ds(start, LANES)])
        tile = jnp.concatenate(parts, axis=0).astype(jnp.float32)
        out_ref[pl.ds(c * LANES, LANES), :] = tile.T.astype(out_ref.dtype)


def pack_rows(coeffs, turn):
    alphas, betas = coeffs.shape
    return pl.pallas_call(
        pack_kernel,
        in_specs=[
            pl.BlockSpec(memory_space=pltpu.SMEM),
            pl.BlockSpec(memory_space=pltpu.VMEM),
        ],
        out_specs=pl.BlockSpec(memory_space=pltpu.VMEM),
        out_shape=jax.ShapeDtypeStruct((alphas * betas // LANES, LANES), coeffs.dtype),
        name="pack_rows",
    )(turn.reshape(1), coeffs)


def table_kernel(chunk, packed_ref, table, stage, spread, sems):
    _, classes, rows, _ = packed_ref.shape
    per_class = rows // chunk
    chunks = classes * per_class
    depth = stage.shape[0]

    def fetch(c, slot):
        start = pl.multiple_of(lax.rem(c, per_class) * chunk, 16)
        return pltpu.make_async_copy(
            packed_ref.at[:, lax.div(c, per_class), pl.ds(start, chunk), :],
            stage.at[slot],
            sems.at[slot],
        )

    for c in range(depth - 1):
        fetch(c, c).start()

    size = 2 * LANES
    source = lax.broadcasted_iota(jnp.int32, (size, size), 0)
    column = lax.broadcasted_iota(jnp.int32, (size, size), 1)
    for m in range(Y // 2):
        turn = 2 * m + (column >> 7)
        wanted = (column & 128) + ((column + 16 * turn) & 127)
        spread[m] = jnp.where(source == wanted, 1.0, 0.0).astype(spread.dtype)
    piece = 256
    lane_part = (lax.broadcasted_iota(jnp.int32, (piece, LANES), 1) >> 4) & 3

    @pl.loop(0, chunks)
    def _(c):
        slot = lax.rem(c, depth)

        @pl.when(c + depth - 1 < chunks)
        def _():
            fetch(c + depth - 1, lax.rem(c + depth - 1, depth)).start()

        fetch(c, slot).wait()
        first = lax.div(c, per_class) * (Y * rows) + lax.rem(c, per_class) * chunk
        for at in range(0, chunk, piece):
            shards = [stage[slot, y, pl.ds(at, piece), :] for y in range(Y)]
            mixed = []
            for g in range(Y):
                rows_g = shards[(Y - 1 - g) % Y]
                for j in range(Y - 1):
                    rows_g = jnp.where(lane_part == j, shards[(j - g) % Y], rows_g)
                mixed.append(rows_g)
            for m in range(Y // 2):
                turned = jnp.dot(
                    jnp.concatenate(mixed[2 * m : 2 * m + 2], axis=1),
                    spread[m],
                    preferred_element_type=jnp.float32,
                )
                for g in (2 * m, 2 * m + 1):
                    to = pl.multiple_of(first + (g * rows + at), 8)
                    lanes = (g - 2 * m) * LANES
                    table[pl.ds(to, piece), :] = turned[:, lanes : lanes + LANES]


def build_table(packed, chunk=768, depth=4):
    _, classes, rows, _ = packed.shape
    pairs = classes * rows * Y
    return pl.pallas_call(
        functools.partial(table_kernel, chunk),
        in_specs=[pl.BlockSpec(memory_space=pl.ANY)],
        out_specs=pl.BlockSpec(memory_space=pltpu.VMEM),
        out_shape=pltpu.VMEM((pairs, LANES), jnp.float32),
        scratch_shapes=[
            pltpu.VMEM((depth, Y, chunk, LANES), jnp.bfloat16),
            pltpu.VMEM((Y // 2, 2 * LANES, 2 * LANES), jnp.bfloat16),
            pltpu.SemaphoreType.DMA((depth,)),
        ],
        compiler_params=pltpu.CompilerParams(vmem_limit_bytes=30 * 2**20),
        cost_estimate=pl.CostEstimate(
            flops=2 * pairs * LANES * Y * LANES, bytes_accessed=packed.size * 2, transcendentals=0
        ),
        name="build_table",
    )(packed)


def pick_kernel(table, idx_ref, w_ref, alpha_ref, out_ref, acc_ref, near, near_sems):
    buffers, batch, slots = near.shape
    targets = w_ref.shape[0]
    rounds = targets // (buffers * batch)

    def bring(r, b):
        start = pl.multiple_of((r * buffers + b) * batch, batch)
        return pltpu.make_async_copy(
            idx_ref.at[pl.ds(start, batch), :], near.at[b], near_sems.at[b]
        )

    for b in range(buffers):
        bring(0, b).start()

    lane_row = lax.broadcasted_iota(jnp.int32, (8, LANES), 0)
    low_lane = lax.broadcasted_iota(jnp.int32, (8, LANES), 1) < LANES // 2

    @pl.loop(0, rounds)
    def _(r):
        for b in range(buffers):
            bring(r, b).wait()
            for g in range(0, batch, 8):
                base = pl.multiple_of((r * buffers + b) * batch + g, 8)
                weights = w_ref[pl.ds(base, 8), :]
                total = jnp.zeros((8, LANES), jnp.float32)
                for q in range(slots):
                    picked = None
                    for k in range(8):
                        row = table[pl.ds(near[b, g + k, q], 1), :]
                        row = jnp.broadcast_to(row, (8, LANES))
                        picked = row if k == 0 else jnp.where(lane_row == k, row, picked)
                    low = jnp.broadcast_to(weights[:, q : q + 1], (8, LANES))
                    high = jnp.broadcast_to(weights[:, slots + q : slots + q + 1], (8, LANES))
                    total = total + picked * jnp.where(low_lane, low, high)
                acc_ref[pl.ds(base, 8), :] = total

            @pl.when(r + 1 < rounds)
            def _():
                bring(r + 1, b).start()

    alphas = out_ref.shape[0]
    for at in range(0, targets, LANES):
        turned = acc_ref[pl.ds(at, LANES), :].T
        beta_term = turned[:alphas, :] + turned[alphas:, :]
        total = alpha_ref[:, pl.ds(at, LANES)] + beta_term
        out_ref[:, pl.ds(at, LANES)] = total.astype(out_ref.dtype)


def sigma_block(table, idx, weights, alpha_term, buffers=2, batch=32):
    targets, slots = idx.shape
    alphas = alpha_term.shape[0]
    table = pltpu.with_memory_space_constraint(table, pltpu.VMEM)
    return pl.pallas_call(
        pick_kernel,
        in_specs=[
            pl.BlockSpec(memory_space=pltpu.VMEM),
            pl.BlockSpec(memory_space=pl.ANY),
            pl.BlockSpec(memory_space=pltpu.VMEM),
            pl.BlockSpec(memory_space=pltpu.VMEM),
        ],
        out_specs=pl.BlockSpec(memory_space=pltpu.VMEM),
        out_shape=jax.ShapeDtypeStruct((alphas, targets), jnp.bfloat16),
        scratch_shapes=[
            pltpu.VMEM((targets, LANES), jnp.float32),
            pltpu.SMEM((buffers, batch, slots), jnp.int32),
            pltpu.SemaphoreType.DMA((buffers,)),
        ],
        compiler_params=pltpu.CompilerParams(vmem_limit_bytes=30 * 2**20),
        cost_estimate=pl.CostEstimate(
            flops=40 * targets * slots * LANES,
            bytes_accessed=40 * targets * slots * LANES,
            transcendentals=0,
        ),
        name="sigma_block",
    )(table, idx, weights, alpha_term)


def per_device(coeffs, alpha_coupling, parent_string_index, excitation_weight):
    own_rows, betas = coeffs.shape
    strings = alpha_coupling.shape[0]
    reps = lax.axis_size("rep")
    cols = lax.axis_size("col")
    parts = reps * Y
    part = betas // parts
    small = part // Z
    along_z = [[y * Z + z for z in range(Z)] for y in range(Y)]
    y_and_col = [[(y * Z + z) * cols + c for y in range(Y) for c in range(cols)] for z in range(Z)]
    row = lax.axis_index("row")
    rep = lax.axis_index("rep")
    mine = (rep * Y + row // Z) * part
    theirs = ((1 - rep) * Y + row // Z) * part

    packed = lax.all_gather(
        pack_rows(coeffs, row // Z), ("row", "col"), axis=0, axis_index_groups=y_and_col
    ).reshape(Y, cols, -1, LANES)

    half = lax.dynamic_slice_in_dim(coeffs, rep * (Y * part), Y * part, 1)
    pieces = half.reshape(own_rows, Y * Z, small).transpose(1, 0, 2)
    columns = lax.all_to_all(pieces, "row", 0, 0).reshape(strings, small)
    alpha_term = jnp.dot(alpha_coupling, columns, preferred_element_type=jnp.float32)
    alpha_term = alpha_term.reshape(Y, Z, own_rows, small).transpose(1, 0, 2, 3)
    alpha_term = lax.all_to_all(alpha_term, "row", 0, 0, axis_index_groups=along_z)
    alpha_term = alpha_term.transpose(1, 2, 0, 3).reshape(Y * own_rows, part)

    sent = jnp.concatenate(
        [
            lax.dynamic_slice_in_dim(parent_string_index, theirs, part, 1).astype(jnp.float32),
            lax.dynamic_slice_in_dim(excitation_weight, theirs, part, 1),
        ],
        axis=0,
    )
    got = lax.ppermute(sent, "rep", [(0, 1), (1, 0)])
    slots = parent_string_index.shape[0]
    idx = jnp.concatenate(
        [
            lax.dynamic_slice_in_dim(parent_string_index, mine, part, 1),
            got[:slots].astype(jnp.int32),
        ],
        axis=0,
    )
    weights = jnp.concatenate(
        [lax.dynamic_slice_in_dim(excitation_weight, mine, part, 1), got[slots:]], axis=0
    )
    halves = idx // (betas // 2)
    upper = (halves & 1) == 1
    idx = (idx - ((halves + 1) >> 1) * (betas // 2)).T
    weights = jnp.concatenate(
        [jnp.where(upper, 0.0, weights), jnp.where(upper, weights, 0.0)], axis=0
    ).T

    table = build_table(packed)
    back = [[r * Y * Z + y * Z + z for r in range(reps) for y in range(Y)] for z in range(Z)]
    calls = 2
    step = part // calls
    done = []
    for c in range(calls):
        at = slice(c * step, (c + 1) * step)
        sigma = sigma_block(table, idx[at], weights[at], alpha_term[:, at])
        if c + 1 < calls:
            sigma, idx = lax.optimization_barrier((sigma, idx))
        pieces = sigma.reshape(Y, own_rows, step)
        pieces = jnp.concatenate([pieces] * reps, axis=0)
        done.append(
            lax.all_to_all(pieces, ("rep", "row"), 0, 0, axis_index_groups=back, tiled=True)
        )
    done = jnp.concatenate(done, axis=2)
    return done.reshape(parts, own_rows, part).transpose(1, 0, 2).reshape(own_rows, betas)


def solution(mesh):
    placed = (P("row", "col"), P(), P("rep", "col"), P("rep", "col"))
    return jax.shard_map(
        per_device, mesh=mesh, in_specs=placed, out_specs=P("row", "col"), check_vma=False
    )
```

```python
import functools

import jax
import jax.numpy as jnp
from jax import lax
from jax.experimental import pallas as pl
from jax.experimental.pallas import tpu as pltpu
from jax.sharding import PartitionSpec as P

Y = 4
Z = 8
LANES = 128


def pack_kernel(turn_ref, in_ref, out_ref):
    alphas, betas = in_ref.shape
    groups = LANES // alphas
    rows = betas // groups
    for c in range(rows // LANES):
        parts = []
        for block in range(groups):
            group = lax.rem(block + groups - turn_ref[0], groups)
            start = pl.multiple_of(group * rows + c * LANES, LANES)
            parts.append(in_ref[:, pl.ds(start, LANES)])
        tile = jnp.concatenate(parts, axis=0).astype(jnp.float32)
        out_ref[pl.ds(c * LANES, LANES), :] = tile.T.astype(out_ref.dtype)


def pack_rows(coeffs, turn):
    alphas, betas = coeffs.shape
    return pl.pallas_call(
        pack_kernel,
        in_specs=[
            pl.BlockSpec(memory_space=pltpu.SMEM),
            pl.BlockSpec(memory_space=pltpu.VMEM),
        ],
        out_specs=pl.BlockSpec(memory_space=pltpu.VMEM),
        out_shape=jax.ShapeDtypeStruct((alphas * betas // LANES, LANES), coeffs.dtype),
        name="pack_rows",
    )(turn.reshape(1), coeffs)


def fill_table(chunk, packed_ref, table, stage, spread, sems):
    _, classes, rows, _ = packed_ref.shape
    per_class = rows // chunk
    chunks = classes * per_class
    depth = stage.shape[0]

    def fetch(c, slot):
        start = pl.multiple_of(lax.rem(c, per_class) * chunk, 16)
        return pltpu.make_async_copy(
            packed_ref.at[:, lax.div(c, per_class), pl.ds(start, chunk), :],
            stage.at[slot],
            sems.at[slot],
        )

    for c in range(depth - 1):
        fetch(c, c).start()

    size = 2 * LANES
    source = lax.broadcasted_iota(jnp.int32, (size, size), 0)
    column = lax.broadcasted_iota(jnp.int32, (size, size), 1)
    for m in range(Y // 2):
        turn = 2 * m + (column >> 7)
        wanted = (column & 128) + ((column + 16 * turn) & 127)
        spread[m] = jnp.where(source == wanted, 1.0, 0.0).astype(spread.dtype)
    piece = 256
    lane_part = (lax.broadcasted_iota(jnp.int32, (piece, LANES), 1) >> 4) & 3

    @pl.loop(0, chunks)
    def _(c):
        slot = lax.rem(c, depth)

        @pl.when(c + depth - 1 < chunks)
        def _():
            fetch(c + depth - 1, lax.rem(c + depth - 1, depth)).start()

        fetch(c, slot).wait()
        first = lax.div(c, per_class) * (Y * rows) + lax.rem(c, per_class) * chunk
        for at in range(0, chunk, piece):
            shards = [stage[slot, y, pl.ds(at, piece), :] for y in range(Y)]
            mixed = []
            for g in range(Y):
                rows_g = shards[(Y - 1 - g) % Y]
                for j in range(Y - 1):
                    rows_g = jnp.where(lane_part == j, shards[(j - g) % Y], rows_g)
                mixed.append(rows_g)
            for m in range(Y // 2):
                turned = jnp.dot(
                    jnp.concatenate(mixed[2 * m : 2 * m + 2], axis=1),
                    spread[m],
                    preferred_element_type=jnp.float32,
                )
                for g in (2 * m, 2 * m + 1):
                    to = pl.multiple_of(first + (g * rows + at), 8)
                    lanes = (g - 2 * m) * LANES
                    table[pl.ds(to, piece), :] = turned[:, lanes : lanes + LANES]


def sigma_kernel(
    chunk,
    idx_ref, w_ref, alpha_ref, packed_ref, out_ref,
    table, stage, spread, acc_ref, near, sems, near_sems,
):
    buffers, batch, slots = near.shape
    targets = w_ref.shape[0]
    rounds = targets // (buffers * batch)

    def bring(r, b):
        start = pl.multiple_of((r * buffers + b) * batch, batch)
        return pltpu.make_async_copy(
            idx_ref.at[pl.ds(start, batch), :], near.at[b], near_sems.at[b]
        )

    for b in range(buffers):
        bring(0, b).start()

    fill_table(chunk, packed_ref, table, stage, spread, sems)

    lane_row = lax.broadcasted_iota(jnp.int32, (8, LANES), 0)
    lane_slot = lax.shift_right_logical(lax.broadcasted_iota(jnp.int32, (8, LANES), 1), 6) * slots

    @pl.loop(0, rounds)
    def _(r):
        for b in range(buffers):
            bring(r, b).wait()
            for g in range(0, batch, 8):
                base = pl.multiple_of((r * buffers + b) * batch + g, 8)
                weights = w_ref[pl.ds(base, 8), :]
                total = jnp.zeros((8, LANES), jnp.float32)
                for q in range(slots):
                    picked = None
                    for k in range(8):
                        row = table[pl.ds(near[b, g + k, q], 1), :]
                        row = jnp.broadcast_to(row, (8, LANES))
                        picked = row if k == 0 else jnp.where(lane_row == k, row, picked)
                    weight = jnp.take_along_axis(
                        weights, lane_slot + q, axis=1, mode="promise_in_bounds"
                    )
                    total = total + picked * weight
                acc_ref[pl.ds(base, 8), :] = total

            @pl.when(r + 1 < rounds)
            def _():
                bring(r + 1, b).start()

    alphas = out_ref.shape[0]
    for at in range(0, targets, LANES):
        turned = acc_ref[pl.ds(at, LANES), :].T
        beta_term = turned[:alphas, :] + turned[alphas:, :]
        total = alpha_ref[:, pl.ds(at, LANES)] + beta_term
        out_ref[:, pl.ds(at, LANES)] = total.astype(out_ref.dtype)


def sigma_block(idx, weights, alpha_term, packed, chunk=768, depth=4, buffers=2, batch=32):
    targets, slots = idx.shape
    alphas = alpha_term.shape[0]
    _, classes, rows, _ = packed.shape
    pairs = classes * rows * Y
    return pl.pallas_call(
        functools.partial(sigma_kernel, chunk),
        in_specs=[
            pl.BlockSpec(memory_space=pl.ANY),
            pl.BlockSpec(memory_space=pltpu.VMEM),
            pl.BlockSpec(memory_space=pltpu.VMEM),
            pl.BlockSpec(memory_space=pl.ANY),
        ],
        out_specs=pl.BlockSpec(memory_space=pltpu.VMEM),
        out_shape=jax.ShapeDtypeStruct((alphas, targets), jnp.bfloat16),
        scratch_shapes=[
            pltpu.VMEM((pairs, LANES), jnp.float32),
            pltpu.VMEM((depth, Y, chunk, LANES), jnp.bfloat16),
            pltpu.VMEM((Y // 2, 2 * LANES, 2 * LANES), jnp.bfloat16),
            pltpu.VMEM((targets, LANES), jnp.float32),
            pltpu.SMEM((buffers, batch, slots), jnp.int32),
            pltpu.SemaphoreType.DMA((depth,)),
            pltpu.SemaphoreType.DMA((buffers,)),
        ],
        compiler_params=pltpu.CompilerParams(vmem_limit_bytes=56 * 2**20),
        cost_estimate=pl.CostEstimate(
            flops=2 * alphas * targets * slots + 2 * pairs * LANES * Y * LANES,
            bytes_accessed=packed.size * 2 + targets * slots * 8 + alphas * targets * 6,
            transcendentals=0,
        ),
        name="sigma_block",
    )(idx, weights, alpha_term, packed)


def per_device(coeffs, alpha_coupling, parent_string_index, excitation_weight):
    own_rows, betas = coeffs.shape
    strings = alpha_coupling.shape[0]
    reps = lax.axis_size("rep")
    cols = lax.axis_size("col")
    parts = reps * Y
    part = betas // parts
    small = part // Z
    along_z = [[y * Z + z for z in range(Z)] for y in range(Y)]
    y_and_col = [[(y * Z + z) * cols + c for y in range(Y) for c in range(cols)] for z in range(Z)]
    row = lax.axis_index("row")
    rep = lax.axis_index("rep")
    mine = (rep * Y + row // Z) * part
    theirs = ((1 - rep) * Y + row // Z) * part

    packed = lax.all_gather(
        pack_rows(coeffs, row // Z), ("row", "col"), axis=0, axis_index_groups=y_and_col
    ).reshape(Y, cols, -1, LANES)

    half = lax.dynamic_slice_in_dim(coeffs, rep * (Y * part), Y * part, 1)
    pieces = half.reshape(own_rows, Y * Z, small).transpose(1, 0, 2)
    columns = lax.all_to_all(pieces, "row", 0, 0).reshape(strings, small)
    alpha_term = jnp.dot(alpha_coupling, columns, preferred_element_type=jnp.float32)
    alpha_term = alpha_term.reshape(Y, Z, own_rows, small).transpose(1, 0, 2, 3)
    alpha_term = lax.all_to_all(alpha_term, "row", 0, 0, axis_index_groups=along_z)
    alpha_term = alpha_term.transpose(1, 2, 0, 3).reshape(Y * own_rows, part)

    sent = jnp.concatenate(
        [
            lax.dynamic_slice_in_dim(parent_string_index, theirs, part, 1).astype(jnp.float32),
            lax.dynamic_slice_in_dim(excitation_weight, theirs, part, 1),
        ],
        axis=0,
    )
    got = lax.ppermute(sent, "rep", [(0, 1), (1, 0)])
    slots = parent_string_index.shape[0]
    idx = jnp.concatenate(
        [
            lax.dynamic_slice_in_dim(parent_string_index, mine, part, 1),
            got[:slots].astype(jnp.int32),
        ],
        axis=0,
    )
    weights = jnp.concatenate(
        [lax.dynamic_slice_in_dim(excitation_weight, mine, part, 1), got[slots:]], axis=0
    )
    halves = idx // (betas // 2)
    upper = (halves & 1) == 1
    idx = (idx - ((halves + 1) >> 1) * (betas // 2)).T
    low, high = jnp.where(upper, 0.0, weights), jnp.where(upper, weights, 0.0)
    weights = jnp.concatenate([low, high] * (LANES // (2 * low.shape[0])), axis=0).T

    sigma = sigma_block(idx, weights, alpha_term, packed)
    pieces = sigma.reshape(Y, own_rows, part)
    pieces = jnp.concatenate([pieces] * reps, axis=0)
    back = [[r * Y * Z + y * Z + z for r in range(reps) for y in range(Y)] for z in range(Z)]
    done = lax.all_to_all(pieces, ("rep", "row"), 0, 0, axis_index_groups=back, tiled=True)
    return done.reshape(parts, own_rows, part).transpose(1, 0, 2).reshape(own_rows, betas)


def solution(mesh):
    placed = (P("row", "col"), P(), P("rep", "col"), P("rep", "col"))
    return jax.shard_map(
        per_device, mesh=mesh, in_specs=placed, out_specs=P("row", "col"), check_vma=False
    )
```

```python
import functools

import jax
import jax.numpy as jnp
from jax import lax
from jax.experimental import pallas as pl
from jax.experimental.pallas import tpu as pltpu
from jax.sharding import PartitionSpec as P

Y = 4
Z = 8
LANES = 128


def pack_kernel(turn_ref, in_ref, out_ref):
    alphas, betas = in_ref.shape
    groups = LANES // alphas
    rows = betas // groups
    for c in range(rows // LANES):
        parts = []
        for block in range(groups):
            group = lax.rem(block + groups - turn_ref[0], groups)
            start = pl.multiple_of(group * rows + c * LANES, LANES)
            parts.append(in_ref[:, pl.ds(start, LANES)])
        tile = jnp.concatenate(parts, axis=0).astype(jnp.float32)
        out_ref[pl.ds(c * LANES, LANES), :] = tile.T.astype(out_ref.dtype)


def pack_rows(coeffs, turn):
    alphas, betas = coeffs.shape
    return pl.pallas_call(
        pack_kernel,
        in_specs=[
            pl.BlockSpec(memory_space=pltpu.SMEM),
            pl.BlockSpec(memory_space=pltpu.VMEM),
        ],
        out_specs=pl.BlockSpec(memory_space=pltpu.VMEM),
        out_shape=jax.ShapeDtypeStruct((alphas * betas // LANES, LANES), coeffs.dtype),
        name="pack_rows",
    )(turn.reshape(1), coeffs)


def fill_table(chunk, packed_ref, table, stage, spread, sems):
    _, classes, rows, _ = packed_ref.shape
    per_class = rows // chunk
    chunks = classes * per_class
    depth = stage.shape[0]

    def fetch(c, slot):
        start = pl.multiple_of(lax.rem(c, per_class) * chunk, 16)
        return pltpu.make_async_copy(
            packed_ref.at[:, lax.div(c, per_class), pl.ds(start, chunk), :],
            stage.at[slot],
            sems.at[slot],
        )

    for c in range(depth - 1):
        fetch(c, c).start()

    size = 2 * LANES
    source = lax.broadcasted_iota(jnp.int32, (size, size), 0)
    column = lax.broadcasted_iota(jnp.int32, (size, size), 1)
    for m in range(Y // 2):
        turn = 2 * m + (column >> 7)
        wanted = (column & 128) + ((column + 16 * turn) & 127)
        spread[m] = jnp.where(source == wanted, 1.0, 0.0).astype(spread.dtype)
    piece = 256
    lane_part = (lax.broadcasted_iota(jnp.int32, (piece, LANES), 1) >> 4) & 3

    @pl.loop(0, chunks)
    def _(c):
        slot = lax.rem(c, depth)

        @pl.when(c + depth - 1 < chunks)
        def _():
            fetch(c + depth - 1, lax.rem(c + depth - 1, depth)).start()

        fetch(c, slot).wait()
        first = lax.div(c, per_class) * (Y * rows) + lax.rem(c, per_class) * chunk
        for at in range(0, chunk, piece):
            shards = [stage[slot, y, pl.ds(at, piece), :] for y in range(Y)]
            mixed = []
            for g in range(Y):
                rows_g = shards[(Y - 1 - g) % Y]
                for j in range(Y - 1):
                    rows_g = jnp.where(lane_part == j, shards[(j - g) % Y], rows_g)
                mixed.append(rows_g)
            for m in range(Y // 2):
                turned = jnp.dot(
                    jnp.concatenate(mixed[2 * m : 2 * m + 2], axis=1),
                    spread[m],
                    preferred_element_type=jnp.float32,
                )
                for g in (2 * m, 2 * m + 1):
                    to = pl.multiple_of(first + (g * rows + at), 8)
                    lanes = (g - 2 * m) * LANES
                    table[pl.ds(to, piece), :] = turned[:, lanes : lanes + LANES]


def sigma_kernel(
    chunk,
    idx_ref, w_ref, alpha_ref, packed_ref, out_ref,
    table, stage, spread, acc_ref, near, sems, near_sems,
):
    buffers, batch, slots = near.shape
    targets = w_ref.shape[0]
    rounds = targets // (buffers * batch)

    def bring(r, b):
        start = pl.multiple_of((r * buffers + b) * batch, batch)
        return pltpu.make_async_copy(
            idx_ref.at[pl.ds(start, batch), :], near.at[b], near_sems.at[b]
        )

    for b in range(buffers):
        bring(0, b).start()

    fill_table(chunk, packed_ref, table, stage, spread, sems)

    lane_row = lax.broadcasted_iota(jnp.int32, (8, LANES), 0)
    lane_slot = lax.shift_right_logical(lax.broadcasted_iota(jnp.int32, (8, LANES), 1), 6) * slots

    @pl.loop(0, rounds)
    def _(r):
        for b in range(buffers):
            bring(r, b).wait()
            for g in range(0, batch, 8):
                base = pl.multiple_of((r * buffers + b) * batch + g, 8)
                weights = w_ref[pl.ds(base, 8), :]
                total = jnp.zeros((8, LANES), jnp.float32)
                for q in range(slots):
                    picked = None
                    for k in range(8):
                        row = table[pl.ds(near[b, g + k, q], 1), :]
                        row = jnp.broadcast_to(row, (8, LANES))
                        picked = row if k == 0 else jnp.where(lane_row == k, row, picked)
                    weight = jnp.take_along_axis(
                        weights, lane_slot + q, axis=1, mode="promise_in_bounds"
                    )
                    total = total + picked * weight
                acc_ref[pl.ds(base, 8), :] = total

            @pl.when(r + 1 < rounds)
            def _():
                bring(r + 1, b).start()

    alphas = alpha_ref.shape[0]
    pieces, piece_rows, _ = out_ref.shape
    for at in range(0, targets, LANES):
        turned = acc_ref[pl.ds(at, LANES), :].T
        beta_term = turned[:alphas, :] + turned[alphas:, :]
        total = (alpha_ref[:, pl.ds(at, LANES)] + beta_term).astype(out_ref.dtype)
        for p in range(pieces):
            first = p * piece_rows % alphas
            out_ref[p, :, pl.ds(at, LANES)] = total[first : first + piece_rows, :]


def sigma_block(pieces, idx, weights, alpha_term, packed, chunk=768, depth=4, buffers=4, batch=16):
    targets, slots = idx.shape
    alphas = alpha_term.shape[0]
    _, classes, rows, _ = packed.shape
    pairs = classes * rows * Y
    return pl.pallas_call(
        functools.partial(sigma_kernel, chunk),
        in_specs=[
            pl.BlockSpec(memory_space=pltpu.VMEM),
            pl.BlockSpec(memory_space=pltpu.VMEM),
            pl.BlockSpec(memory_space=pltpu.VMEM),
            pl.BlockSpec(memory_space=pl.ANY),
        ],
        out_specs=pl.BlockSpec(memory_space=pltpu.VMEM),
        out_shape=jax.ShapeDtypeStruct((pieces, alphas // Y, targets), jnp.bfloat16),
        scratch_shapes=[
            pltpu.VMEM((pairs, LANES), jnp.float32),
            pltpu.VMEM((depth, Y, chunk, LANES), jnp.bfloat16),
            pltpu.VMEM((Y // 2, 2 * LANES, 2 * LANES), jnp.bfloat16),
            pltpu.VMEM((targets, LANES), jnp.float32),
            pltpu.SMEM((buffers, batch, slots), jnp.int32),
            pltpu.SemaphoreType.DMA((depth,)),
            pltpu.SemaphoreType.DMA((buffers,)),
        ],
        compiler_params=pltpu.CompilerParams(vmem_limit_bytes=52 * 2**20),
        cost_estimate=pl.CostEstimate(
            flops=2 * alphas * targets * slots + 2 * pairs * LANES * Y * LANES,
            bytes_accessed=packed.size * 2 + targets * slots * 8 + alphas * targets * 6,
            transcendentals=0,
        ),
        name="sigma_block",
    )(idx, weights, alpha_term, packed)


def per_device(coeffs, alpha_coupling, parent_string_index, excitation_weight):
    own_rows, betas = coeffs.shape
    strings = alpha_coupling.shape[0]
    reps = lax.axis_size("rep")
    cols = lax.axis_size("col")
    parts = reps * Y
    part = betas // parts
    small = part // Z
    along_z = [[y * Z + z for z in range(Z)] for y in range(Y)]
    y_and_col = [[(y * Z + z) * cols + c for y in range(Y) for c in range(cols)] for z in range(Z)]
    row = lax.axis_index("row")
    rep = lax.axis_index("rep")
    mine = (rep * Y + row // Z) * part
    theirs = ((1 - rep) * Y + row // Z) * part

    packed = lax.all_gather(
        pack_rows(coeffs, row // Z), ("row", "col"), axis=0, axis_index_groups=y_and_col
    ).reshape(Y, cols, -1, LANES)

    half = lax.dynamic_slice_in_dim(coeffs, rep * (Y * part), Y * part, 1)
    pieces = half.reshape(own_rows, Y * Z, small).transpose(1, 0, 2)
    columns = lax.all_to_all(pieces, "row", 0, 0).reshape(strings, small)
    alpha_term = jnp.dot(alpha_coupling, columns, preferred_element_type=jnp.float32)
    alpha_term = alpha_term.reshape(Y, Z, own_rows, small).transpose(1, 0, 2, 3)
    alpha_term = lax.all_to_all(alpha_term, "row", 0, 0, axis_index_groups=along_z)
    alpha_term = alpha_term.transpose(1, 2, 0, 3).reshape(Y * own_rows, part)

    sent = jnp.concatenate(
        [
            lax.dynamic_slice_in_dim(parent_string_index, theirs, part, 1).astype(jnp.float32),
            lax.dynamic_slice_in_dim(excitation_weight, theirs, part, 1),
        ],
        axis=0,
    )
    got = lax.ppermute(sent, "rep", [(0, 1), (1, 0)])
    slots = parent_string_index.shape[0]
    idx = jnp.concatenate(
        [
            lax.dynamic_slice_in_dim(parent_string_index, mine, part, 1),
            got[:slots].astype(jnp.int32),
        ],
        axis=0,
    )
    weights = jnp.concatenate(
        [lax.dynamic_slice_in_dim(excitation_weight, mine, part, 1), got[slots:]], axis=0
    )
    halves = idx // (betas // 2)
    upper = (halves & 1) == 1
    idx = (idx - ((halves + 1) >> 1) * (betas // 2)).T
    low, high = jnp.where(upper, 0.0, weights), jnp.where(upper, weights, 0.0)
    weights = jnp.concatenate([low, high] * (LANES // (2 * low.shape[0])), axis=0).T

    pieces = sigma_block(reps * Y, idx, weights, alpha_term, packed)
    back = [[r * Y * Z + y * Z + z for r in range(reps) for y in range(Y)] for z in range(Z)]
    done = lax.all_to_all(pieces, ("rep", "row"), 0, 0, axis_index_groups=back, tiled=True)
    return done.reshape(parts, own_rows, part).transpose(1, 0, 2).reshape(own_rows, betas)


def solution(mesh):
    placed = (P("row", "col"), P(), P("rep", "col"), P("rep", "col"))
    return jax.shard_map(
        per_device, mesh=mesh, in_specs=placed, out_specs=P("row", "col"), check_vma=False
    )
```

```python
import functools

import jax
import jax.numpy as jnp
from jax import lax
from jax.experimental import pallas as pl
from jax.experimental.pallas import tpu as pltpu
from jax.sharding import PartitionSpec as P

Y = 4
Z = 8
LANES = 128


def pack_kernel(turn_ref, in_ref, out_ref):
    alphas, betas = in_ref.shape
    groups = LANES // alphas
    rows = betas // groups
    for c in range(rows // LANES):
        parts = []
        for block in range(groups):
            group = lax.rem(block + groups - turn_ref[0], groups)
            start = pl.multiple_of(group * rows + c * LANES, LANES)
            parts.append(in_ref[:, pl.ds(start, LANES)])
        tile = jnp.concatenate(parts, axis=0).astype(jnp.float32)
        out_ref[pl.ds(c * LANES, LANES), :] = tile.T.astype(out_ref.dtype)


def pack_rows(coeffs, turn):
    alphas, betas = coeffs.shape
    return pl.pallas_call(
        pack_kernel,
        in_specs=[
            pl.BlockSpec(memory_space=pltpu.SMEM),
            pl.BlockSpec(memory_space=pltpu.VMEM),
        ],
        out_specs=pl.BlockSpec(memory_space=pltpu.VMEM),
        out_shape=jax.ShapeDtypeStruct((alphas * betas // LANES, LANES), coeffs.dtype),
        name="pack_rows",
    )(turn.reshape(1), coeffs)


def fill_table(chunk, packed_ref, table, stage, spread, sems):
    _, classes, rows, _ = packed_ref.shape
    per_class = rows // chunk
    chunks = classes * per_class
    depth = stage.shape[0]

    def fetch(c, slot):
        start = pl.multiple_of(lax.rem(c, per_class) * chunk, 16)
        return pltpu.make_async_copy(
            packed_ref.at[:, lax.div(c, per_class), pl.ds(start, chunk), :],
            stage.at[slot],
            sems.at[slot],
        )

    for c in range(depth - 1):
        fetch(c, c).start()

    size = 2 * LANES
    source = lax.broadcasted_iota(jnp.int32, (size, size), 0)
    column = lax.broadcasted_iota(jnp.int32, (size, size), 1)
    for m in range(Y // 2):
        turn = 2 * m + (column >> 7)
        wanted = (column & 128) + ((column + 16 * turn) & 127)
        spread[m] = jnp.where(source == wanted, 1.0, 0.0).astype(spread.dtype)
    piece = 256
    lane_part = (lax.broadcasted_iota(jnp.int32, (piece, LANES), 1) >> 4) & 3

    @pl.loop(0, chunks)
    def _(c):
        slot = lax.rem(c, depth)

        @pl.when(c + depth - 1 < chunks)
        def _():
            fetch(c + depth - 1, lax.rem(c + depth - 1, depth)).start()

        fetch(c, slot).wait()
        first = lax.div(c, per_class) * (Y * rows) + lax.rem(c, per_class) * chunk
        for at in range(0, chunk, piece):
            shards = [stage[slot, y, pl.ds(at, piece), :] for y in range(Y)]
            mixed = []
            for g in range(Y):
                rows_g = shards[(Y - 1 - g) % Y]
                for j in range(Y - 1):
                    rows_g = jnp.where(lane_part == j, shards[(j - g) % Y], rows_g)
                mixed.append(rows_g)
            for m in range(Y // 2):
                turned = jnp.dot(
                    jnp.concatenate(mixed[2 * m : 2 * m + 2], axis=1),
                    spread[m],
                    preferred_element_type=jnp.float32,
                )
                for g in (2 * m, 2 * m + 1):
                    to = pl.multiple_of(first + (g * rows + at), 8)
                    lanes = (g - 2 * m) * LANES
                    table[pl.ds(to, piece), :] = turned[:, lanes : lanes + LANES]


def sigma_kernel(
    chunk,
    idx_ref, w_ref, alpha_ref, packed_ref, out_ref,
    table, stage, spread, acc_ref, near, sems, near_sems,
):
    buffers, index_rows, _ = near.shape
    targets = w_ref.shape[0]
    batch = targets // idx_ref.shape[0]
    slots = index_rows * LANES // batch
    rounds = targets // (buffers * batch)

    def bring(r, b):
        return pltpu.make_async_copy(idx_ref.at[r * buffers + b], near.at[b], near_sems.at[b])

    for b in range(buffers):
        bring(0, b).start()

    fill_table(chunk, packed_ref, table, stage, spread, sems)

    lane_row = lax.broadcasted_iota(jnp.int32, (8, LANES), 0)
    lane_slot = lax.shift_right_logical(lax.broadcasted_iota(jnp.int32, (8, LANES), 1), 6) * slots

    @pl.loop(0, rounds)
    def _(r):
        for b in range(buffers):
            bring(r, b).wait()
            for g in range(0, batch, 8):
                base = pl.multiple_of((r * buffers + b) * batch + g, 8)
                weights = w_ref[pl.ds(base, 8), :]
                total = jnp.zeros((8, LANES), jnp.float32)
                for q in range(slots):
                    picked = None
                    for k in range(8):
                        at = (g + k) * slots + q
                        row = table[pl.ds(near[b, at // LANES, at % LANES], 1), :]
                        row = jnp.broadcast_to(row, (8, LANES))
                        picked = row if k == 0 else jnp.where(lane_row == k, row, picked)
                    weight = jnp.take_along_axis(
                        weights, lane_slot + q, axis=1, mode="promise_in_bounds"
                    )
                    total = total + picked * weight
                acc_ref[pl.ds(base, 8), :] = total

            @pl.when(r + 1 < rounds)
            def _():
                bring(r + 1, b).start()

    alphas = alpha_ref.shape[0]
    pieces, piece_rows, _ = out_ref.shape
    for at in range(0, targets, LANES):
        turned = acc_ref[pl.ds(at, LANES), :].T
        beta_term = turned[:alphas, :] + turned[alphas:, :]
        total = (alpha_ref[:, pl.ds(at, LANES)] + beta_term).astype(out_ref.dtype)
        for p in range(pieces):
            first = p * piece_rows % alphas
            out_ref[p, :, pl.ds(at, LANES)] = total[first : first + piece_rows, :]


def sigma_block(pieces, idx, weights, alpha_term, packed, chunk=768, depth=4, buffers=4, batch=16):
    targets, slots = idx.shape
    idx = idx.reshape(targets // batch, batch * slots // LANES, LANES)
    alphas = alpha_term.shape[0]
    _, classes, rows, _ = packed.shape
    pairs = classes * rows * Y
    return pl.pallas_call(
        functools.partial(sigma_kernel, chunk),
        in_specs=[
            pl.BlockSpec(memory_space=pltpu.VMEM),
            pl.BlockSpec(memory_space=pltpu.VMEM),
            pl.BlockSpec(memory_space=pltpu.VMEM),
            pl.BlockSpec(memory_space=pl.ANY),
        ],
        out_specs=pl.BlockSpec(memory_space=pltpu.VMEM),
        out_shape=jax.ShapeDtypeStruct((pieces, alphas // Y, targets), jnp.bfloat16),
        scratch_shapes=[
            pltpu.VMEM((pairs, LANES), jnp.float32),
            pltpu.VMEM((depth, Y, chunk, LANES), jnp.bfloat16),
            pltpu.VMEM((Y // 2, 2 * LANES, 2 * LANES), jnp.bfloat16),
            pltpu.VMEM((targets, LANES), jnp.float32),
            pltpu.SMEM((buffers, *idx.shape[1:]), jnp.int32),
            pltpu.SemaphoreType.DMA((depth,)),
            pltpu.SemaphoreType.DMA((buffers,)),
        ],
        compiler_params=pltpu.CompilerParams(vmem_limit_bytes=52 * 2**20),
        cost_estimate=pl.CostEstimate(
            flops=2 * alphas * targets * slots + 2 * pairs * LANES * Y * LANES,
            bytes_accessed=packed.size * 2 + targets * slots * 8 + alphas * targets * 6,
            transcendentals=0,
        ),
        name="sigma_block",
    )(idx, weights, alpha_term, packed)


def per_device(coeffs, alpha_coupling, parent_string_index, excitation_weight):
    own_rows, betas = coeffs.shape
    strings = alpha_coupling.shape[0]
    reps = lax.axis_size("rep")
    cols = lax.axis_size("col")
    parts = reps * Y
    part = betas // parts
    small = part // Z
    along_z = [[y * Z + z for z in range(Z)] for y in range(Y)]
    y_and_col = [[(y * Z + z) * cols + c for y in range(Y) for c in range(cols)] for z in range(Z)]
    row = lax.axis_index("row")
    rep = lax.axis_index("rep")
    mine = (rep * Y + row // Z) * part
    theirs = ((1 - rep) * Y + row // Z) * part

    packed = lax.all_gather(
        pack_rows(coeffs, row // Z), ("row", "col"), axis=0, axis_index_groups=y_and_col
    ).reshape(Y, cols, -1, LANES)

    half = lax.dynamic_slice_in_dim(coeffs, rep * (Y * part), Y * part, 1)
    pieces = half.reshape(own_rows, Y * Z, small).transpose(1, 0, 2)
    columns = lax.all_to_all(pieces, "row", 0, 0).reshape(strings, small)
    alpha_term = jnp.dot(alpha_coupling, columns, preferred_element_type=jnp.float32)
    alpha_term = alpha_term.reshape(Y, Z, own_rows, small).transpose(1, 0, 2, 3)
    alpha_term = lax.all_to_all(alpha_term, "row", 0, 0, axis_index_groups=along_z)
    alpha_term = alpha_term.transpose(1, 2, 0, 3).reshape(Y * own_rows, part)

    sent = jnp.concatenate(
        [
            lax.dynamic_slice_in_dim(parent_string_index, theirs, part, 1).astype(jnp.float32),
            lax.dynamic_slice_in_dim(excitation_weight, theirs, part, 1),
        ],
        axis=0,
    )
    got = lax.ppermute(sent, "rep", [(0, 1), (1, 0)])
    slots = parent_string_index.shape[0]
    idx = jnp.concatenate(
        [
            lax.dynamic_slice_in_dim(parent_string_index, mine, part, 1),
            got[:slots].astype(jnp.int32),
        ],
        axis=0,
    )
    weights = jnp.concatenate(
        [lax.dynamic_slice_in_dim(excitation_weight, mine, part, 1), got[slots:]], axis=0
    )
    halves = idx // (betas // 2)
    upper = (halves & 1) == 1
    idx = (idx - ((halves + 1) >> 1) * (betas // 2)).T
    low, high = jnp.where(upper, 0.0, weights), jnp.where(upper, weights, 0.0)
    weights = jnp.concatenate([low, high] * (LANES // (2 * low.shape[0])), axis=0).T

    pieces = sigma_block(reps * Y, idx, weights, alpha_term, packed)
    back = [[r * Y * Z + y * Z + z for r in range(reps) for y in range(Y)] for z in range(Z)]
    done = lax.all_to_all(pieces, ("rep", "row"), 0, 0, axis_index_groups=back, tiled=True)
    return done.reshape(parts, own_rows, part).transpose(1, 0, 2).reshape(own_rows, betas)


def solution(mesh):
    placed = (P("row", "col"), P(), P("rep", "col"), P("rep", "col"))
    return jax.shard_map(
        per_device, mesh=mesh, in_specs=placed, out_specs=P("row", "col"), check_vma=False
    )
```

```python
import functools

import jax
import jax.numpy as jnp
from jax import lax
from jax.experimental import pallas as pl
from jax.experimental.pallas import tpu as pltpu
from jax.sharding import PartitionSpec as P

Y = 4
Z = 8
LANES = 128


def pack_kernel(turn_ref, in_ref, out_ref):
    alphas, betas = in_ref.shape
    groups = LANES // alphas
    rows = betas // groups
    for c in range(rows // LANES):
        parts = []
        for block in range(groups):
            group = lax.rem(block + groups - turn_ref[0], groups)
            start = pl.multiple_of(group * rows + c * LANES, LANES)
            parts.append(in_ref[:, pl.ds(start, LANES)])
        tile = jnp.concatenate(parts, axis=0).astype(jnp.float32)
        out_ref[pl.ds(c * LANES, LANES), :] = tile.T.astype(out_ref.dtype)


def pack_rows(coeffs, turn):
    alphas, betas = coeffs.shape
    return pl.pallas_call(
        pack_kernel,
        in_specs=[
            pl.BlockSpec(memory_space=pltpu.SMEM),
            pl.BlockSpec(memory_space=pltpu.VMEM),
        ],
        out_specs=pl.BlockSpec(memory_space=pltpu.VMEM),
        out_shape=jax.ShapeDtypeStruct((alphas * betas // LANES, LANES), coeffs.dtype),
        name="pack_rows",
    )(turn.reshape(1), coeffs)


def fill_table(chunk, packed_ref, table, stage, spread, sems):
    _, classes, rows, _ = packed_ref.shape
    per_class = rows // chunk
    chunks = classes * per_class
    depth = stage.shape[0]

    def fetch(c, slot):
        start = pl.multiple_of(lax.rem(c, per_class) * chunk, 16)
        return pltpu.make_async_copy(
            packed_ref.at[:, lax.div(c, per_class), pl.ds(start, chunk), :],
            stage.at[slot],
            sems.at[slot],
        )

    for c in range(depth - 1):
        fetch(c, c).start()

    size = 2 * LANES
    source = lax.broadcasted_iota(jnp.int32, (size, size), 0)
    column = lax.broadcasted_iota(jnp.int32, (size, size), 1)
    for m in range(Y // 2):
        turn = 2 * m + (column >> 7)
        wanted = (column & 128) + ((column + 16 * turn) & 127)
        spread[m] = jnp.where(source == wanted, 1.0, 0.0).astype(spread.dtype)
    piece = 256
    lane_part = (lax.broadcasted_iota(jnp.int32, (piece, LANES), 1) >> 4) & 3

    @pl.loop(0, chunks)
    def _(c):
        slot = lax.rem(c, depth)

        @pl.when(c + depth - 1 < chunks)
        def _():
            fetch(c + depth - 1, lax.rem(c + depth - 1, depth)).start()

        fetch(c, slot).wait()
        first = lax.div(c, per_class) * (Y * rows) + lax.rem(c, per_class) * chunk
        for at in range(0, chunk, piece):
            shards = [stage[slot, y, pl.ds(at, piece), :] for y in range(Y)]
            mixed = []
            for g in range(Y):
                rows_g = shards[(Y - 1 - g) % Y]
                for j in range(Y - 1):
                    rows_g = jnp.where(lane_part == j, shards[(j - g) % Y], rows_g)
                mixed.append(rows_g)
            for m in range(Y // 2):
                turned = jnp.dot(
                    jnp.concatenate(mixed[2 * m : 2 * m + 2], axis=1),
                    spread[m],
                    preferred_element_type=jnp.float32,
                )
                for g in (2 * m, 2 * m + 1):
                    to = pl.multiple_of(first + (g * rows + at), 8)
                    lanes = (g - 2 * m) * LANES
                    table[pl.ds(to, piece), :] = turned[:, lanes : lanes + LANES]


def sigma_kernel(
    chunk,
    idx_ref, w_ref, alpha_ref, packed_ref, out_ref,
    table, stage, spread, acc_ref, near, sems, near_sems,
):
    buffers, index_rows, _ = near.shape
    targets = w_ref.shape[0]
    batch = targets // idx_ref.shape[0]
    slots = index_rows * LANES // batch
    rounds = targets // (buffers * batch)

    def bring(r, b):
        return pltpu.make_async_copy(idx_ref.at[r * buffers + b], near.at[b], near_sems.at[b])

    for b in range(buffers):
        bring(0, b).start()

    fill_table(chunk, packed_ref, table, stage, spread, sems)

    lane_row = lax.broadcasted_iota(jnp.int32, (8, LANES), 0)
    lane_slot = lax.shift_right_logical(lax.broadcasted_iota(jnp.int32, (8, LANES), 1), 6) * slots

    @pl.loop(0, rounds)
    def _(r):
        for b in range(buffers):
            bring(r, b).wait()
            for g in range(0, batch, 8):
                base = pl.multiple_of((r * buffers + b) * batch + g, 8)
                weights = w_ref[pl.ds(base, 8), :]
                total = jnp.zeros((8, LANES), jnp.float32)
                for q in range(slots):
                    picked = None
                    for k in range(8):
                        at = (g + k) * slots + q
                        row = table[pl.ds(near[b, at // LANES, at % LANES], 1), :]
                        row = jnp.broadcast_to(row, (8, LANES))
                        picked = row if k == 0 else jnp.where(lane_row == k, row, picked)
                    weight = jnp.take_along_axis(
                        weights, lane_slot + q, axis=1, mode="promise_in_bounds"
                    )
                    total = total + picked * weight
                acc_ref[pl.ds(base, 8), :] = total

            @pl.when(r + 1 < rounds)
            def _():
                bring(r + 1, b).start()

    alphas = alpha_ref.shape[0]
    pieces, piece_rows, _ = out_ref.shape
    for at in range(0, targets, LANES):
        turned = acc_ref[pl.ds(at, LANES), :].T
        beta_term = turned[:alphas, :] + turned[alphas:, :]
        total = (alpha_ref[:, pl.ds(at, LANES)] + beta_term).astype(out_ref.dtype)
        for p in range(pieces):
            first = p * piece_rows % alphas
            out_ref[p, :, pl.ds(at, LANES)] = total[first : first + piece_rows, :]


def sigma_block(pieces, idx, weights, alpha_term, packed, chunk=768, depth=4, buffers=4, batch=16):
    targets, slots = idx.shape
    idx = idx.reshape(targets // batch, batch * slots // LANES, LANES)
    alphas = alpha_term.shape[0]
    _, classes, rows, _ = packed.shape
    pairs = classes * rows * Y
    return pl.pallas_call(
        functools.partial(sigma_kernel, chunk),
        in_specs=[
            pl.BlockSpec(memory_space=pltpu.VMEM),
            pl.BlockSpec(memory_space=pltpu.VMEM),
            pl.BlockSpec(memory_space=pltpu.VMEM),
            pl.BlockSpec(memory_space=pl.ANY),
        ],
        out_specs=pl.BlockSpec(memory_space=pltpu.VMEM),
        out_shape=jax.ShapeDtypeStruct((pieces, alphas // Y, targets), jnp.bfloat16),
        scratch_shapes=[
            pltpu.VMEM((pairs, LANES), jnp.float32),
            pltpu.VMEM((depth, Y, chunk, LANES), jnp.bfloat16),
            pltpu.VMEM((Y // 2, 2 * LANES, 2 * LANES), jnp.bfloat16),
            pltpu.VMEM((targets, LANES), jnp.float32),
            pltpu.SMEM((buffers, *idx.shape[1:]), jnp.int32),
            pltpu.SemaphoreType.DMA((depth,)),
            pltpu.SemaphoreType.DMA((buffers,)),
        ],
        compiler_params=pltpu.CompilerParams(vmem_limit_bytes=52 * 2**20),
        cost_estimate=pl.CostEstimate(
            flops=2 * alphas * targets * slots + 2 * pairs * LANES * Y * LANES,
            bytes_accessed=packed.size * 2 + targets * slots * 8 + alphas * targets * 6,
            transcendentals=0,
        ),
        name="sigma_block",
    )(idx, weights, alpha_term, packed)


def per_device(coeffs, alpha_coupling, parent_string_index, excitation_weight):
    own_rows, betas = coeffs.shape
    strings = alpha_coupling.shape[0]
    reps = lax.axis_size("rep")
    cols = lax.axis_size("col")
    parts = reps * Y
    part = betas // parts
    small = part // Z
    along_z = [[y * Z + z for z in range(Z)] for y in range(Y)]
    y_and_col = [[(y * Z + z) * cols + c for y in range(Y) for c in range(cols)] for z in range(Z)]
    row = lax.axis_index("row")
    rep = lax.axis_index("rep")
    mine = (rep * Y + row // Z) * part
    theirs = ((1 - rep) * Y + row // Z) * part

    packed = lax.all_gather(
        pack_rows(coeffs, row // Z), ("row", "col"), axis=0, axis_index_groups=y_and_col
    ).reshape(Y, cols, -1, LANES)

    half = lax.dynamic_slice_in_dim(coeffs, rep * (Y * part), Y * part, 1)
    pieces = half.reshape(own_rows, Y * Z, small).transpose(1, 0, 2)
    columns = lax.all_to_all(pieces, "row", 0, 0).reshape(strings, small)
    alpha_term = jnp.dot(alpha_coupling, columns, preferred_element_type=jnp.float32)
    alpha_term = alpha_term.reshape(Y, Z, own_rows, small).transpose(1, 0, 2, 3)
    alpha_term = lax.all_to_all(alpha_term, "row", 0, 0, axis_index_groups=along_z)
    alpha_term = alpha_term.transpose(1, 2, 0, 3).reshape(Y * own_rows, part)

    sent = jnp.concatenate(
        [
            lax.dynamic_slice_in_dim(parent_string_index, theirs, part, 1).astype(jnp.float32),
            lax.dynamic_slice_in_dim(excitation_weight, theirs, part, 1),
        ],
        axis=0,
    )
    got = lax.ppermute(sent, "rep", [(0, 1), (1, 0)])
    slots = parent_string_index.shape[0]
    idx = jnp.concatenate(
        [
            lax.dynamic_slice_in_dim(parent_string_index, mine, part, 1),
            got[:slots].astype(jnp.int32),
        ],
        axis=0,
    )
    weights = jnp.concatenate(
        [lax.dynamic_slice_in_dim(excitation_weight, mine, part, 1), got[slots:]], axis=0
    )
    halves = idx // (betas // 2)
    upper = (halves & 1) == 1
    idx = (idx - ((halves + 1) >> 1) * (betas // 2)).T
    low, high = jnp.where(upper, 0.0, weights), jnp.where(upper, weights, 0.0)
    weights = jnp.concatenate([low, high] * (LANES // (2 * low.shape[0])), axis=0).T

    pieces = sigma_block(Y, idx, weights, alpha_term, packed)
    passed = lax.ppermute(pieces, "rep", [(0, 1), (1, 0)])
    along_y = [[y * Z + z for y in range(Y)] for z in range(Z)]
    here = lax.all_to_all(pieces, "row", 0, 0, axis_index_groups=along_y)
    there = lax.all_to_all(passed, "row", 0, 0, axis_index_groups=along_y)
    first, second = jnp.where(rep == 0, here, there), jnp.where(rep == 0, there, here)
    done = jnp.concatenate([first, second], axis=0)
    return done.transpose(1, 0, 2).reshape(own_rows, betas)


def solution(mesh):
    placed = (P("row", "col"), P(), P("rep", "col"), P("rep", "col"))
    return jax.shard_map(
        per_device, mesh=mesh, in_specs=placed, out_specs=P("row", "col"), check_vma=False
    )
```
